32 devices in a mesh: grp: 2 (over y), aux: 4 (over z), occ: 4 (over x, core).
Axes of the slice: x: 2, y: 2, z: 4, core: 2. Of those that a mesh axis runs over, the one named last changes fastest.
Arguments:
- b_factors: bfloat16 [16, 960, 512], P(('grp', 'occ'), 'aux'), parts along dimension 0, may hold values from -2.5 to 2.5
- tile_mask: int32 [16, 8], P('grp'), parts along dimension 0, may hold values 0 or 1
- batch_list: int32 [16], P('grp'), parts along dimension 0, may hold values from 0 to 499, as said below
- occ_energy: float32 [500], replicated, may hold values from -2 to -0.3
- vir_energy: float32 [512], P('aux'), may hold values from 0.2 to 4
Outputs:
- gamma: float32 [16, 960, 512], P(('grp', 'occ'), 'aux'), parts along dimension 0
The draws below stay inside these ranges and needn't reach their ends.
There are 2 independent parts, one for each index of `grp`. The reference program is written for one: setup_inputs(seed, part) draws one part's arguments, and reference() takes and returns one part's arrays. A program takes and returns all parts, laid end to end along the dimension named above; an argument that names none is the same for every part. Nothing has to cross between parts.
Inputs may be any that keep to these rules, and one draw needn't show every extreme that they name: `batch_list`: entries are distinct; the first and the last occupied orbital of the molecule are always among them.
All inputs are finite; a program needn't handle non-finite values.
Results may differ from the reference program's by a relative error of at most 0.002.
Values may be sent and summed in bfloat16 or wider, within the bound.
A program may use at most 128 MiB of HBM per device.

```python
import jax
import jax.numpy as jnp
from jax import lax

VBLK = 128
TILE = 64
NOCC_ALL = 500
NAUX = 960
NVIR = 512
NVT = 8
NOB = 8
N_AUX = 4


def draw_batch_list(key, part):
    key = jax.random.fold_in(key, 1)
    first_key, second_key = jax.random.split(key)
    middle = jax.random.permutation(first_key, NOCC_ALL - 2)[:NOB - 2].astype(jnp.int32) + 1
    ends = jnp.array([0, NOCC_ALL - 1], dtype=jnp.int32)
    chosen = jnp.concatenate([ends, middle])
    order = jax.random.permutation(second_key, NOB)
    return chosen[order].astype(jnp.int32)


def set_ends(entries, stream_key, low, high):
    longest = entries.shape.index(max(entries.shape))
    spots = []
    for shift in (0, 1):
        where = [jax.random.randint(jax.random.fold_in(stream_key, axis), (), 0, length) for axis, length in enumerate(entries.shape)]
        where[longest] = (where[longest] + shift) % entries.shape[longest]
        spots.append(tuple(where))
    return entries.at[spots[0]].set(low).at[spots[1]].set(high)


def levels(stream_key, extent, pieces, least, high):
    def one(dim, shards_of):
        draws = jax.random.uniform(jax.random.fold_in(jax.random.fold_in(stream_key, 6), dim), (shards_of,), jnp.float32, least / len(pieces), high / len(pieces))
        return jnp.repeat(jnp.exp(draws), extent[dim] // shards_of).reshape((-1,) + (1,) * (len(extent) - dim - 1))

    gain = one(*pieces[0])
    for cut in pieces[1:]:
        gain = gain * one(*cut)
    return gain


def gaussian(stream_key, shape, width, limit, pieces=(), kind=jnp.bfloat16):
    drawn = width * jax.random.normal(stream_key, shape, jnp.float32)
    if pieces:
        drawn = drawn * levels(stream_key, shape, pieces, -0.22, 0.18)
    return jnp.clip(drawn, -limit, limit).astype(kind)


def setup_inputs(seed: int = 0, part: int = 0) -> dict:
    splits = jax.random.split(jax.random.key(seed), 6)
    part_splits = jax.random.split(jax.random.fold_in(splits[5], part), 6)
    b_factors = gaussian(part_splits[0], (NOB, NAUX, NVIR), (NAUX ** -0.25), 2.5, ((0, 4), (1, 4)))
    tile_mask = set_ends((jax.random.randint(part_splits[1], (NOB, NVT), 0, 4) < 3).astype(jnp.int32), jax.random.fold_in(part_splits[1], 1), 0, 1)
    batch_list = draw_batch_list(jax.random.fold_in(jax.random.fold_in(splits[5], part), 71), part)
    occ_energy = jnp.clip(jax.random.uniform(splits[3], (NOCC_ALL,), jnp.float32, -2.0, -0.3), -2.0, -0.3)
    vir_energy = jnp.clip(0.2 + 3.8 * jax.random.uniform(splits[4], (NVIR,), jnp.float32) ** levels(splits[4], (NVIR,), ((0, 4),), -0.2, 0.2), 0.2, 4.0)
    return dict(b_factors=b_factors, tile_mask=tile_mask, batch_list=batch_list, occ_energy=occ_energy, vir_energy=vir_energy)


def pair_weights(coulomb, energy_mine, energy_other, energy_vir, mask_mine, mask_other):
    denominator = (energy_mine[:, None, None, None] + energy_other[None, None, :, None]
                   - energy_vir[None, :, None, None] - energy_vir[None, None, None, :])
    amplitude = coulomb * mask_mine[:, :, None, None] * mask_other[None, None, :, :] / denominator
    combined = 2.0 * amplitude - jnp.swapaxes(amplitude, 1, 3)
    return combined.astype(jnp.bfloat16)


def reference(b_factors, tile_mask, batch_list, occ_energy, vir_energy):
    hits = batch_list[:, None] == jnp.arange(NOCC_ALL, dtype=jnp.int32)[None, :]
    energy_batch = jnp.sum(jnp.where(hits, occ_energy[None, :], jnp.float32(0.0)), axis=1)
    vir_mask = jnp.repeat(tile_mask.astype(jnp.float32), TILE, axis=1)

    def domain(domain_number):
        offset = (domain_number * VBLK).astype(jnp.int32)
        factors = lax.dynamic_slice_in_dim(b_factors, offset, VBLK, 2).astype(jnp.float32)
        masked = lax.dynamic_slice_in_dim(vir_mask, offset, VBLK, 1)
        energy_dom = lax.dynamic_slice_in_dim(vir_energy, offset, VBLK, 0)
        coulomb = jnp.einsum("iqa,jqb->iajb", factors, factors)
        weights = pair_weights(coulomb, energy_batch, energy_batch, energy_dom, masked, masked)
        weights = lax.optimization_barrier(weights).astype(jnp.float32)
        return jnp.einsum("iajb,jqb->iqa", weights, factors)

    blocks = lax.map(domain, jnp.arange(N_AUX, dtype=jnp.int32))
    return jnp.transpose(blocks, (1, 2, 0, 3)).reshape(NOB, NAUX, NVIR)
```

```python
import functools

import jax
import jax.numpy as jnp
from jax import lax
from jax.experimental import pallas as pl
from jax.experimental.pallas import tpu as pltpu
from jax.sharding import PartitionSpec as P

VBLK = 128
TILE = 64
OCC = 4


def flip(index, bits):
    bit = 1
    while bit <= bits:
        if bits & bit:
            index = index + bit - 2 * bit * (lax.div(index, bit) % 2)
        bit *= 2
    return index


def send_order(n):
    return [k for k in range(1, n) if 2 * k >= n] + [k for k in range(1, n) if 2 * k < n]


def kernel(
    n,
    b_ref,
    tile_ref,
    batch_ref,
    occ_ref,
    vir_ref,
    out_ref,
    gath,
    coul,
    w_dir,
    w_exc,
    amp,
    outgoing,
    incoming,
    own_sem,
    z_send,
    z_recv,
    f_send,
    f_recv,
    r_send,
    r_recv,
):
    own = b_ref.shape[0]
    width = own * VBLK
    z = lax.axis_index("aux")
    o = lax.axis_index("occ")
    zs = [flip(z, k) for k in range(n)]
    os = [flip(o, r) for r in range(OCC)]

    def columns(k):
        return pl.ds(pl.multiple_of(zs[k] * VBLK, VBLK), VBLK)

    def remote(src, dst, send_sem, recv_sem, **where):
        return pltpu.make_async_remote_copy(
            src_ref=src,
            dst_ref=dst,
            send_sem=send_sem,
            recv_sem=recv_sem,
            device_id=where,
            device_id_type=pl.DeviceIdType.MESH,
        )

    own_copy = pltpu.make_async_copy(b_ref.at[:, :, columns(0)], gath.at[0, 0], own_sem)
    own_copy.start()

    barrier = pltpu.get_barrier_semaphore()
    for k in range(1, n):
        pl.semaphore_signal(barrier, inc=1, device_id={"aux": zs[k]}, device_id_type=pl.DeviceIdType.MESH)
    for r in (1, 2):
        pl.semaphore_signal(barrier, inc=1, device_id={"occ": os[r]}, device_id_type=pl.DeviceIdType.MESH)
    pl.semaphore_wait(barrier, n + 1)

    far_first = send_order(n)
    z_copies = {}
    for k in far_first:
        z_copies[k] = remote(b_ref.at[:, :, columns(k)], gath.at[0, k], z_send.at[k], z_recv.at[k], aux=zs[k])
        z_copies[k].start()
    near = [remote(gath.at[0, k], gath.at[1, k], f_send.at[0, k], f_recv.at[0, k], occ=os[1]) for k in range(n)]
    cross = [remote(gath.at[0, k], gath.at[2, k], f_send.at[1, k], f_recv.at[1, k], occ=os[2]) for k in range(n)]
    onward = [remote(gath.at[2, k], gath.at[3, k], f_send.at[2, k], f_recv.at[2, k], occ=os[1]) for k in range(n)]

    own_copy.wait()
    cross[0].start()
    near[0].start()

    orbitals = [[os[r] * own + i for i in range(own)] for r in range(OCC)]
    energy = [[occ_ref[batch_ref[j]] for j in row] for row in orbitals]
    tiles = VBLK // TILE
    mask = [
        [[tile_ref[j, z * tiles + t].astype(jnp.float32) for t in range(tiles)] for j in row] for row in orbitals
    ]
    lane_tile = lax.broadcasted_iota(jnp.int32, (1, VBLK), 1) // TILE

    def row_mask(values):
        row = jnp.full((1, VBLK), values[0], jnp.float32)
        for t in range(1, tiles):
            row = jnp.where(lane_tile == t, values[t], row)
        return row

    rows = [[row_mask(m) for m in entry] for entry in mask]
    vir = jnp.broadcast_to(vir_ref[...], (VBLK, VBLK))
    vir_sum = vir + vir.T
    for r in range(OCC):
        for jj in range(own):
            for i in range(own):
                inverse = 1.0 / ((energy[0][i] + energy[r][jj]) - vir_sum)
                for t in range(tiles):
                    part = inverse[t * TILE : (t + 1) * TILE]
                    at = pl.ds((r * own + jj) * VBLK + t * TILE, TILE)
                    to = pl.ds(i * VBLK, VBLK)
                    w_dir[at, to] = part * (rows[0][i] * (2.0 * mask[r][jj][t]))
                    w_exc[at, to] = part * (rows[r][jj] * mask[0][i][t])

    def wide(r, k):
        return jnp.concatenate([gath[r, k, i] for i in range(own)], axis=1)

    def add_chunk(k, first):
        mine = wide(0, k)
        for r in range(OCC):
            term = lax.dot_general(
                mine, wide(r, k), (((0,), (0,)), ((), ())), preferred_element_type=jnp.float32
            )
            at = pl.ds(r * width, width)
            if first:
                coul[:, at] = term
            else:
                coul[:, at] += term

    order = [0] + far_first[::-1]
    for step in range(n + 2):
        if 0 < step < n:
            k = order[step]
            z_copies[k].wait_recv()
            cross[k].start()
            near[k].start()
        if 1 <= step < n + 1:
            k = order[step - 1]
            cross[k].wait_recv()
            onward[k].start()
        if step >= 2:
            k = order[step - 2]
            near[k].wait_recv()
            onward[k].wait_recv()
            add_chunk(k, step == 2)

    for r in range(OCC):
        for jj in range(own):
            for i in range(own):
                block = coul[pl.ds(i * VBLK, VBLK), pl.ds((r * own + jj) * VBLK, VBLK)]
                at = pl.ds((r * own + jj) * VBLK, VBLK)
                to = pl.ds(i * VBLK, VBLK)
                amp[at, to] = (block.T * w_dir[at, to] - block * w_exc[at, to]).astype(jnp.bfloat16)

    def density(k):
        total = jnp.dot(wide(0, k), amp[pl.ds(0, width)], preferred_element_type=jnp.float32)
        for r in range(1, OCC):
            total += jnp.dot(wide(r, k), amp[pl.ds(r * width, width)], preferred_element_type=jnp.float32)
        return total

    back = {}
    for k in far_first:
        total = density(k)
        for i in range(own):
            outgoing[k, i] = total[:, i * VBLK : (i + 1) * VBLK].astype(jnp.bfloat16)
        back[k] = remote(outgoing.at[k], incoming.at[k], r_send.at[k], r_recv.at[k], aux=zs[k])
        back[k].start()
    total = density(0)
    for i in range(own):
        out_ref[i, :, columns(0)] = total[:, i * VBLK : (i + 1) * VBLK]

    for k in far_first[::-1]:
        back[k].wait_recv()
        for i in range(own):
            out_ref[i, :, columns(k)] = incoming[k, i].astype(jnp.float32)

    for k in range(n):
        near[k].wait_send()
        cross[k].wait_send()
        onward[k].wait_send()
        if k:
            z_copies[k].wait_send()
            back[k].wait_send()


def shards(n, b_factors, tile_mask, batch_list, occ_energy, vir_energy):
    own, depth, columns = b_factors.shape
    width = own * VBLK
    dma = pltpu.SemaphoreType.DMA
    chunk = (own, depth, VBLK)
    chunk_bytes = own * depth * VBLK * 2
    pair_bytes = OCC * width * width * 4
    need = (OCC + 2) * n * chunk_bytes + 4 * pair_bytes + 2 * n * chunk_bytes
    vmem = pl.BlockSpec(memory_space=pltpu.VMEM)
    smem = pl.BlockSpec(memory_space=pltpu.SMEM)
    return pl.pallas_call(
        functools.partial(kernel, n),
        out_shape=jax.ShapeDtypeStruct(b_factors.shape, jnp.float32),
        in_specs=[pl.BlockSpec(memory_space=pl.ANY), smem, smem, smem, vmem],
        out_specs=vmem,
        scratch_shapes=[
            pltpu.VMEM((OCC, n) + chunk, jnp.bfloat16),
            pltpu.VMEM((width, OCC * width), jnp.float32),
            pltpu.VMEM((OCC * width, width), jnp.float32),
            pltpu.VMEM((OCC * width, width), jnp.float32),
            pltpu.VMEM((OCC * width, width), jnp.bfloat16),
            pltpu.VMEM((n,) + chunk, jnp.bfloat16),
            pltpu.VMEM((n,) + chunk, jnp.bfloat16),
            dma,
            dma((n,)),
            dma((n,)),
            dma((3, n)),
            dma((3, n)),
            dma((n,)),
            dma((n,)),
        ],
        compiler_params=pltpu.CompilerParams(
            collective_id=0, has_side_effects=True, vmem_limit_bytes=need + (12 << 20)
        ),
    )(b_factors, tile_mask, batch_list, occ_energy, vir_energy[None, :])


def solution(mesh):
    in_specs = (P(("grp", "occ"), "aux", None), P("grp", None), P("grp"), P(), P("aux"))
    out_specs = P(("grp", "occ"), "aux", None)
    return jax.shard_map(
        functools.partial(shards, mesh.shape["aux"]), mesh=mesh, in_specs=in_specs, out_specs=out_specs, check_vma=False
    )
```

```python
import functools

import jax
import jax.numpy as jnp
from jax import lax
from jax.experimental import pallas as pl
from jax.experimental.pallas import tpu as pltpu
from jax.sharding import PartitionSpec as P

VBLK = 128
TILE = 64
OCC = 4


def flip(index, bits):
    bit = 1
    while bit <= bits:
        if bits & bit:
            index = index + bit - 2 * bit * (lax.div(index, bit) % 2)
        bit *= 2
    return index


def send_order(n):
    return [k for k in range(1, n) if 2 * k >= n] + [k for k in range(1, n) if 2 * k < n]


def kernel(
    n,
    b_ref,
    tile_hbm,
    batch_hbm,
    occ_hbm,
    vir_hbm,
    out_ref,
    tile_ref,
    batch_ref,
    occ_ref,
    vir_ref,
    gath,
    coul,
    w_dir,
    w_exc,
    amp,
    outgoing,
    incoming,
    own_sem,
    small_sem,
    z_send,
    z_recv,
    f_send,
    f_recv,
    r_send,
    r_recv,
    result,
    store_sem,
):
    own = b_ref.shape[0]
    width = own * VBLK
    z = lax.axis_index("aux")
    o = lax.axis_index("occ")
    zs = [flip(z, k) for k in range(n)]
    os = [flip(o, r) for r in range(OCC)]

    def columns(k):
        return pl.ds(pl.multiple_of(zs[k] * VBLK, VBLK), VBLK)

    def remote(src, dst, send_sem, recv_sem, **where):
        return pltpu.make_async_remote_copy(
            src_ref=src,
            dst_ref=dst,
            send_sem=send_sem,
            recv_sem=recv_sem,
            device_id=where,
            device_id_type=pl.DeviceIdType.MESH,
        )

    own_copy = pltpu.make_async_copy(b_ref.at[:, :, columns(0)], gath.at[0, 0], own_sem)
    small = [
        pltpu.make_async_copy(src, dst, small_sem.at[j])
        for j, (src, dst) in enumerate(
            ((tile_hbm, tile_ref), (batch_hbm, batch_ref), (occ_hbm, occ_ref), (vir_hbm, vir_ref))
        )
    ]
    own_copy.start()
    for copy in small:
        copy.start()

    barrier = pltpu.get_barrier_semaphore()
    for k in range(1, n):
        pl.semaphore_signal(barrier, inc=1, device_id={"aux": zs[k]}, device_id_type=pl.DeviceIdType.MESH)
    for r in (1, 2):
        pl.semaphore_signal(barrier, inc=1, device_id={"occ": os[r]}, device_id_type=pl.DeviceIdType.MESH)
    pl.semaphore_wait(barrier, n + 1)

    far_first = send_order(n)
    order = [0] + far_first[::-1]
    pieces = [(k, i) for k in order for i in range(own)]
    z_copies = {}
    for k, i in pieces[own:]:
        z_copies[k, i] = remote(
            b_ref.at[i, :, columns(k)], gath.at[0, k, i], z_send.at[k, i], z_recv.at[k, i], aux=zs[k]
        )
        z_copies[k, i].start()

    def passing(kind, source, target, partner):
        return {
            (k, i): remote(
                gath.at[source, k, i], gath.at[target, k, i], f_send.at[kind, k, i], f_recv.at[kind, k, i], occ=os[partner]
            )
            for k, i in pieces
        }

    near = passing(0, 0, 1, 1)
    cross = passing(1, 0, 2, 2)
    onward = passing(2, 2, 3, 1)

    own_copy.wait()
    for i in range(own):
        cross[0, i].start()
    for i in range(own):
        near[0, i].start()
    for copy in small:
        copy.wait()

    orbitals = [[os[r] * own + i for i in range(own)] for r in range(OCC)]
    energy = [[occ_ref[batch_ref[j]] for j in row] for row in orbitals]
    tiles = VBLK // TILE
    mask = [
        [[tile_ref[j, z * tiles + t].astype(jnp.float32) for t in range(tiles)] for j in row] for row in orbitals
    ]
    lane_tile = lax.broadcasted_iota(jnp.int32, (1, VBLK), 1) // TILE

    def row_mask(values):
        row = jnp.full((1, VBLK), values[0], jnp.float32)
        for t in range(1, tiles):
            row = jnp.where(lane_tile == t, values[t], row)
        return row

    rows = [[row_mask(m) for m in entry] for entry in mask]
    vir = jnp.broadcast_to(vir_ref[...], (VBLK, VBLK))
    vir_sum = vir + vir.T
    for r in range(OCC):
        for jj in range(own):
            for i in range(own):
                inverse = 1.0 / ((energy[0][i] + energy[r][jj]) - vir_sum)
                for t in range(tiles):
                    part = inverse[t * TILE : (t + 1) * TILE]
                    at = pl.ds((r * own + jj) * VBLK + t * TILE, TILE)
                    to = pl.ds(i * VBLK, VBLK)
                    w_dir[at, to] = part * (rows[0][i] * (2.0 * mask[r][jj][t]))
                    w_exc[at, to] = part * (rows[r][jj] * mask[0][i][t])

    def wide(r, k):
        return jnp.concatenate([gath[r, k, i] for i in range(own)], axis=1)

    def add_chunk(k, first):
        mine = wide(0, k)
        for r in range(OCC):
            term = lax.dot_general(
                mine, wide(r, k), (((0,), (0,)), ((), ())), preferred_element_type=jnp.float32
            )
            at = pl.ds(r * width, width)
            if first:
                coul[:, at] = term
            else:
                coul[:, at] += term

    lag = own
    for step in range(len(pieces) + 2 * lag):
        if own <= step < len(pieces):
            piece = pieces[step]
            z_copies[piece].wait_recv()
            cross[piece].start()
            near[piece].start()
        if lag <= step < len(pieces) + lag:
            piece = pieces[step - lag]
            cross[piece].wait_recv()
            onward[piece].start()
        if step >= 2 * lag:
            piece = pieces[step - 2 * lag]
            near[piece].wait_recv()
            onward[piece].wait_recv()
            if piece[1] == own - 1:
                add_chunk(piece[0], piece[0] == 0)

    for r in range(OCC):
        for jj in range(own):
            for i in range(own):
                block = coul[pl.ds(i * VBLK, VBLK), pl.ds((r * own + jj) * VBLK, VBLK)]
                at = pl.ds((r * own + jj) * VBLK, VBLK)
                to = pl.ds(i * VBLK, VBLK)
                amp[at, to] = (block.T * w_dir[at, to] - block * w_exc[at, to]).astype(jnp.bfloat16)

    def density(k):
        total = jnp.dot(wide(0, k), amp[pl.ds(0, width)], preferred_element_type=jnp.float32)
        for r in range(1, OCC):
            total += jnp.dot(wide(r, k), amp[pl.ds(r * width, width)], preferred_element_type=jnp.float32)
        return total

    stores = [
        pltpu.make_async_copy(result.at[k], out_ref.at[:, :, columns(k)], store_sem.at[k]) for k in range(n)
    ]
    back = {}
    for k in far_first:
        total = density(k)
        for i in range(own):
            outgoing[k, i] = total[:, i * VBLK : (i + 1) * VBLK].astype(jnp.bfloat16)
        back[k] = remote(outgoing.at[k], incoming.at[k], r_send.at[k], r_recv.at[k], aux=zs[k])
        back[k].start()
    total = density(0)
    for i in range(own):
        result[0, i] = total[:, i * VBLK : (i + 1) * VBLK]
    stores[0].start()

    for k in far_first[::-1]:
        back[k].wait_recv()
        for i in range(own):
            result[k, i] = incoming[k, i].astype(jnp.float32)
        stores[k].start()

    for piece in pieces:
        near[piece].wait_send()
        cross[piece].wait_send()
        onward[piece].wait_send()
        if piece[0]:
            z_copies[piece].wait_send()
    for k in far_first:
        back[k].wait_send()
    for copy in stores:
        copy.wait()


def shards(n, b_factors, tile_mask, batch_list, occ_energy, vir_energy):
    own, depth, columns = b_factors.shape
    width = own * VBLK
    dma = pltpu.SemaphoreType.DMA
    chunk = (own, depth, VBLK)
    chunk_bytes = own * depth * VBLK * 2
    pair_bytes = OCC * width * width * 4
    need = (OCC + 2) * n * chunk_bytes + 4 * pair_bytes + 2 * n * chunk_bytes
    hbm = pl.BlockSpec(memory_space=pltpu.HBM)
    return pl.pallas_call(
        functools.partial(kernel, n),
        out_shape=jax.ShapeDtypeStruct(b_factors.shape, jnp.float32),
        in_specs=[hbm] * 5,
        out_specs=hbm,
        scratch_shapes=[
            pltpu.SMEM(tile_mask.shape, jnp.int32),
            pltpu.SMEM(batch_list.shape, jnp.int32),
            pltpu.SMEM(occ_energy.shape, jnp.float32),
            pltpu.VMEM((1, VBLK), jnp.float32),
            pltpu.VMEM((OCC, n) + chunk, jnp.bfloat16),
            pltpu.VMEM((width, OCC * width), jnp.float32),
            pltpu.VMEM((OCC * width, width), jnp.float32),
            pltpu.VMEM((OCC * width, width), jnp.float32),
            pltpu.VMEM((OCC * width, width), jnp.bfloat16),
            pltpu.VMEM((n,) + chunk, jnp.bfloat16),
            pltpu.VMEM((n,) + chunk, jnp.bfloat16),
            dma,
            dma((4,)),
            dma((n, own)),
            dma((n, own)),
            dma((3, n, own)),
            dma((3, n, own)),
            dma((n,)),
            dma((n,)),
            pltpu.VMEM((n,) + chunk, jnp.float32),
            dma((n,)),
        ],
        compiler_params=pltpu.CompilerParams(
            collective_id=0, has_side_effects=True, vmem_limit_bytes=58000 << 10
        ),
    )(b_factors, tile_mask, batch_list, occ_energy, vir_energy[None, :])


def solution(mesh):
    in_specs = (P(("grp", "occ"), "aux", None), P("grp", None), P("grp"), P(), P("aux"))
    out_specs = P(("grp", "occ"), "aux", None)
    return jax.shard_map(
        functools.partial(shards, mesh.shape["aux"]), mesh=mesh, in_specs=in_specs, out_specs=out_specs, check_vma=False
    )
```

```python
import functools

import jax
import jax.numpy as jnp
from jax import lax
from jax.experimental import pallas as pl
from jax.experimental.pallas import tpu as pltpu
from jax.sharding import PartitionSpec as P

VBLK = 128
TILE = 64
OCC = 4


def flip(index, bits):
    bit = 1
    while bit <= bits:
        if bits & bit:
            index = index + bit - 2 * bit * (lax.div(index, bit) % 2)
        bit *= 2
    return index


def send_order(n):
    return [k for k in range(1, n) if 2 * k >= n] + [k for k in range(1, n) if 2 * k < n]


def kernel(
    n,
    b_ref,
    tile_hbm,
    batch_hbm,
    occ_hbm,
    vir_hbm,
    out_ref,
    tile_ref,
    batch_ref,
    occ_ref,
    vir_ref,
    gath,
    coul,
    w_dir,
    w_exc,
    amp,
    outgoing,
    own_sem,
    small_sem,
    z_send,
    z_recv,
    f_send,
    f_recv,
    r_send,
    r_recv,
    store_sem,
):
    own = b_ref.shape[0]
    width = own * VBLK
    z = lax.axis_index("aux")
    o = lax.axis_index("occ")
    zs = [flip(z, k) for k in range(n)]
    os = [flip(o, r) for r in range(OCC)]

    def columns(k):
        return pl.ds(pl.multiple_of(zs[k] * VBLK, VBLK), VBLK)

    def remote(src, dst, send_sem, recv_sem, **where):
        return pltpu.make_async_remote_copy(
            src_ref=src,
            dst_ref=dst,
            send_sem=send_sem,
            recv_sem=recv_sem,
            device_id=where,
            device_id_type=pl.DeviceIdType.MESH,
        )

    barrier = pltpu.get_barrier_semaphore()
    for k in range(1, n):
        pl.semaphore_signal(barrier, inc=1, device_id={"aux": zs[k]}, device_id_type=pl.DeviceIdType.MESH)
    for r in (1, 2):
        pl.semaphore_signal(barrier, inc=1, device_id={"occ": os[r]}, device_id_type=pl.DeviceIdType.MESH)

    own_copy = pltpu.make_async_copy(b_ref.at[:, :, columns(0)], gath.at[0, 0], own_sem)
    small = [
        pltpu.make_async_copy(src, dst, small_sem.at[j])
        for j, (src, dst) in enumerate(
            ((tile_hbm, tile_ref), (batch_hbm, batch_ref), (occ_hbm, occ_ref), (vir_hbm, vir_ref))
        )
    ]
    own_copy.start()
    for copy in small:
        copy.start()
    pl.semaphore_wait(barrier, n + 1)

    far_first = send_order(n)
    order = [0] + far_first[::-1]
    pieces = [(k, i) for k in order for i in range(own)]
    z_copies = {}
    for k, i in pieces[own:]:
        z_copies[k, i] = remote(
            b_ref.at[i, :, columns(k)], gath.at[0, k, i], z_send.at[k, i], z_recv.at[k, i], aux=zs[k]
        )
        z_copies[k, i].start()

    def passing(kind, source, target, partner):
        return {
            (k, i): remote(
                gath.at[source, k, i], gath.at[target, k, i], f_send.at[kind, k, i], f_recv.at[kind, k, i], occ=os[partner]
            )
            for k, i in pieces
        }

    near = passing(0, 0, 1, 1)
    cross = passing(1, 0, 2, 2)
    onward = passing(2, 2, 3, 1)

    own_copy.wait()
    for i in range(own):
        cross[0, i].start()
    for i in range(own):
        near[0, i].start()
    for copy in small:
        copy.wait()

    orbitals = [[os[r] * own + i for i in range(own)] for r in range(OCC)]
    energy = [[occ_ref[batch_ref[j]] for j in row] for row in orbitals]
    tiles = VBLK // TILE
    mask = [
        [[tile_ref[j, z * tiles + t].astype(jnp.float32) for t in range(tiles)] for j in row] for row in orbitals
    ]
    lane_tile = lax.broadcasted_iota(jnp.int32, (1, VBLK), 1) // TILE

    def row_mask(values):
        row = jnp.full((1, VBLK), values[0], jnp.float32)
        for t in range(1, tiles):
            row = jnp.where(lane_tile == t, values[t], row)
        return row

    rows = [[row_mask(m) for m in entry] for entry in mask]
    vir = jnp.broadcast_to(vir_ref[...], (VBLK, VBLK))
    vir_sum = vir + vir.T
    for r in range(OCC):
        for jj in range(own):
            for i in range(own):
                inverse = 1.0 / ((energy[0][i] + energy[r][jj]) - vir_sum)
                for t in range(tiles):
                    part = inverse[t * TILE : (t + 1) * TILE]
                    at = pl.ds((r * own + jj) * VBLK + t * TILE, TILE)
                    to = pl.ds(i * VBLK, VBLK)
                    w_dir[at, to] = part * (rows[0][i] * (2.0 * mask[r][jj][t]))
                    w_exc[at, to] = part * (rows[r][jj] * mask[0][i][t])

    def wide(r, k):
        return jnp.concatenate([gath[r, k, i] for i in range(own)], axis=1)

    def add_chunk(k, first):
        mine = wide(0, k)
        for r in range(OCC):
            term = lax.dot_general(
                mine, wide(r, k), (((0,), (0,)), ((), ())), preferred_element_type=jnp.float32
            )
            at = pl.ds(r * width, width)
            if first:
                coul[:, at] = term
            else:
                coul[:, at] += term

    lag = own
    for step in range(len(pieces) + 2 * lag):
        if own <= step < len(pieces):
            piece = pieces[step]
            z_copies[piece].wait_recv()
            cross[piece].start()
            near[piece].start()
        if lag <= step < len(pieces) + lag:
            piece = pieces[step - lag]
            cross[piece].wait_recv()
            onward[piece].start()
        if step >= 2 * lag:
            piece = pieces[step - 2 * lag]
            near[piece].wait_recv()
            onward[piece].wait_recv()
            if piece[1] == own - 1:
                add_chunk(piece[0], piece[0] == 0)

    for r in range(OCC):
        for jj in range(own):
            for i in range(own):
                block = coul[pl.ds(i * VBLK, VBLK), pl.ds((r * own + jj) * VBLK, VBLK)]
                at = pl.ds((r * own + jj) * VBLK, VBLK)
                to = pl.ds(i * VBLK, VBLK)
                amp[at, to] = (block.T * w_dir[at, to] - block * w_exc[at, to]).astype(jnp.bfloat16)

    def density(k):
        total = jnp.dot(wide(0, k), amp[pl.ds(0, width)], preferred_element_type=jnp.float32)
        for r in range(1, OCC):
            total += jnp.dot(wide(r, k), amp[pl.ds(r * width, width)], preferred_element_type=jnp.float32)
        return total

    back = {}
    for k in far_first:
        total = density(k)
        for i in range(own):
            outgoing[k, i] = total[:, i * VBLK : (i + 1) * VBLK].astype(jnp.bfloat16)
        back[k] = remote(outgoing.at[k], out_ref.at[z], r_send.at[k], r_recv.at[k], aux=zs[k])
        back[k].start()
    total = density(0)
    for i in range(own):
        outgoing[0, i] = total[:, i * VBLK : (i + 1) * VBLK].astype(jnp.bfloat16)
    store = pltpu.make_async_copy(outgoing.at[0], out_ref.at[z], store_sem)
    store.start()

    for k in far_first[::-1]:
        back[k].wait_recv()

    for piece in pieces:
        near[piece].wait_send()
        cross[piece].wait_send()
        onward[piece].wait_send()
        if piece[0]:
            z_copies[piece].wait_send()
    for k in far_first:
        back[k].wait_send()
    store.wait()


def shards(n, b_factors, tile_mask, batch_list, occ_energy, vir_energy):
    own, depth, columns = b_factors.shape
    width = own * VBLK
    dma = pltpu.SemaphoreType.DMA
    chunk = (own, depth, VBLK)
    chunk_bytes = own * depth * VBLK * 2
    pair_bytes = OCC * width * width * 4
    need = (OCC + 2) * n * chunk_bytes + 4 * pair_bytes + 2 * n * chunk_bytes
    hbm = pl.BlockSpec(memory_space=pltpu.HBM)
    slots = pl.pallas_call(
        functools.partial(kernel, n),
        out_shape=jax.ShapeDtypeStruct((n,) + chunk, jnp.bfloat16),
        in_specs=[hbm] * 5,
        out_specs=hbm,
        scratch_shapes=[
            pltpu.SMEM(tile_mask.shape, jnp.int32),
            pltpu.SMEM(batch_list.shape, jnp.int32),
            pltpu.SMEM(occ_energy.shape, jnp.float32),
            pltpu.VMEM((1, VBLK), jnp.float32),
            pltpu.VMEM((OCC, n) + chunk, jnp.bfloat16),
            pltpu.VMEM((width, OCC * width), jnp.float32),
            pltpu.VMEM((OCC * width, width), jnp.float32),
            pltpu.VMEM((OCC * width, width), jnp.float32),
            pltpu.VMEM((OCC * width, width), jnp.bfloat16),
            pltpu.VMEM((n,) + chunk, jnp.bfloat16),
            dma,
            dma((4,)),
            dma((n, own)),
            dma((n, own)),
            dma((3, n, own)),
            dma((3, n, own)),
            dma((n,)),
            dma((n,)),
            dma,
        ],
        compiler_params=pltpu.CompilerParams(
            collective_id=0, has_side_effects=True, vmem_limit_bytes=58000 << 10
        ),
    )(b_factors, tile_mask, batch_list, occ_energy, vir_energy[None, :])
    return jnp.concatenate([slots[k].astype(jnp.float32) for k in range(n)], axis=2)


def solution(mesh):
    in_specs = (P(("grp", "occ"), "aux", None), P("grp", None), P("grp"), P(), P("aux"))
    out_specs = P(("grp", "occ"), "aux", None)
    return jax.shard_map(
        functools.partial(shards, mesh.shape["aux"]), mesh=mesh, in_specs=in_specs, out_specs=out_specs, check_vma=False
    )
```

```python
import functools

import jax
import jax.numpy as jnp
from jax import lax
from jax.experimental import pallas as pl
from jax.experimental.pallas import tpu as pltpu
from jax.sharding import PartitionSpec as P

VBLK = 128
TILE = 64
OCC = 4


def flip(index, bits):
    bit = 1
    while bit <= bits:
        if bits & bit:
            index = index + bit - 2 * bit * (lax.div(index, bit) % 2)
        bit *= 2
    return index


def send_order(n):
    return [k for k in range(1, n) if 2 * k >= n] + [k for k in range(1, n) if 2 * k < n]


def kernel(
    n,
    b_ref,
    tile_hbm,
    batch_hbm,
    occ_hbm,
    vir_hbm,
    out_ref,
    tile_ref,
    batch_ref,
    occ_ref,
    vir_ref,
    gath,
    coul,
    w_dir,
    w_exc,
    amp,
    outgoing,
    own_sem,
    small_sem,
    z_send,
    z_recv,
    f_send,
    f_recv,
    r_send,
    r_recv,
    store_sem,
):
    own = b_ref.shape[0]
    width = own * VBLK
    z = lax.axis_index("aux")
    o = lax.axis_index("occ")
    zs = [flip(z, k) for k in range(n)]
    os = [flip(o, r) for r in range(OCC)]

    def columns(k):
        return pl.ds(pl.multiple_of(zs[k] * VBLK, VBLK), VBLK)

    def remote(src, dst, send_sem, recv_sem, **where):
        return pltpu.make_async_remote_copy(
            src_ref=src,
            dst_ref=dst,
            send_sem=send_sem,
            recv_sem=recv_sem,
            device_id=where,
            device_id_type=pl.DeviceIdType.MESH,
        )

    barrier = pltpu.get_barrier_semaphore()
    for k in range(1, n):
        pl.semaphore_signal(barrier, inc=1, device_id={"aux": zs[k]}, device_id_type=pl.DeviceIdType.MESH)
    for r in (1, 2):
        pl.semaphore_signal(barrier, inc=1, device_id={"occ": os[r]}, device_id_type=pl.DeviceIdType.MESH)

    own_copy = pltpu.make_async_copy(b_ref.at[:, :, columns(0)], gath.at[0, 0], own_sem)
    small = [
        pltpu.make_async_copy(src, dst, small_sem.at[j])
        for j, (src, dst) in enumerate(
            ((tile_hbm, tile_ref), (batch_hbm, batch_ref), (occ_hbm, occ_ref), (vir_hbm, vir_ref))
        )
    ]
    own_copy.start()
    for copy in small:
        copy.start()
    pl.semaphore_wait(barrier, n + 1)

    far_first = send_order(n)
    order = [0] + far_first[::-1]
    pieces = [(k, i) for k in order for i in range(own)]
    z_copies = {}
    for k, i in pieces[own:]:
        z_copies[k, i] = remote(
            b_ref.at[i, :, columns(k)], gath.at[0, k, i], z_send.at[k, i], z_recv.at[k, i], aux=zs[k]
        )
        z_copies[k, i].start()

    def passing(kind, source, target, partner):
        return {
            (k, i): remote(
                gath.at[source, k, i], gath.at[target, k, i], f_send.at[kind, k, i], f_recv.at[kind, k, i], occ=os[partner]
            )
            for k, i in pieces
        }

    near = passing(0, 0, 1, 1)
    cross = passing(1, 0, 2, 2)
    onward = passing(2, 2, 3, 1)

    own_copy.wait()
    for i in range(own):
        cross[0, i].start()
    for i in range(own):
        near[0, i].start()
    for copy in small:
        copy.wait()

    orbitals = [[os[r] * own + i for i in range(own)] for r in range(OCC)]
    energy = [[occ_ref[batch_ref[j]] for j in row] for row in orbitals]
    tiles = VBLK // TILE
    mask = [
        [[tile_ref[j, z * tiles + t].astype(jnp.float32) for t in range(tiles)] for j in row] for row in orbitals
    ]
    lane_tile = lax.broadcasted_iota(jnp.int32, (1, VBLK), 1) // TILE

    def row_mask(values):
        row = jnp.full((1, VBLK), values[0], jnp.float32)
        for t in range(1, tiles):
            row = jnp.where(lane_tile == t, values[t], row)
        return row

    rows = [[row_mask(m) for m in entry] for entry in mask]
    vir = jnp.broadcast_to(vir_ref[...], (VBLK, VBLK))
    vir_sum = vir + vir.T
    for r in range(OCC):
        for jj in range(own):
            for i in range(own):
                inverse = 1.0 / ((energy[0][i] + energy[r][jj]) - vir_sum)
                for t in range(tiles):
                    part = inverse[t * TILE : (t + 1) * TILE]
                    at = pl.ds((r * own + jj) * VBLK + t * TILE, TILE)
                    to = pl.ds(i * VBLK, VBLK)
                    w_dir[at, to] = part * (rows[0][i] * (2.0 * mask[r][jj][t]))
                    w_exc[at, to] = part * (rows[r][jj] * mask[0][i][t])

    def wide(r, k):
        return jnp.concatenate([gath[r, k, i] for i in range(own)], axis=1)

    def add_chunk(k, first):
        mine = wide(0, k)
        for r in range(OCC):
            term = lax.dot_general(
                mine, wide(r, k), (((0,), (0,)), ((), ())), preferred_element_type=jnp.float32
            )
            at = pl.ds(r * width, width)
            if first:
                coul[:, at] = term
            else:
                coul[:, at] += term

    lag = own
    for step in range(len(pieces) + 2 * lag):
        if own <= step < len(pieces):
            piece = pieces[step]
            z_copies[piece].wait_recv()
            cross[piece].start()
        if lag <= step < len(pieces) + lag:
            piece = pieces[step - lag]
            if piece[0]:
                near[piece].start()
            cross[piece].wait_recv()
            onward[piece].start()
        if step >= 2 * lag:
            piece = pieces[step - 2 * lag]
            near[piece].wait_recv()
            onward[piece].wait_recv()
            if piece[1] == own - 1:
                add_chunk(piece[0], piece[0] == 0)

    for r in range(OCC):
        for jj in range(own):
            for i in range(own):
                block = coul[pl.ds(i * VBLK, VBLK), pl.ds((r * own + jj) * VBLK, VBLK)]
                at = pl.ds((r * own + jj) * VBLK, VBLK)
                to = pl.ds(i * VBLK, VBLK)
                amp[at, to] = (block.T * w_dir[at, to] - block * w_exc[at, to]).astype(jnp.bfloat16)

    def density(k, rows):
        def part(r):
            return jnp.concatenate([gath[r, k, i, rows] for i in range(own)], axis=1)

        total = jnp.dot(part(0), amp[pl.ds(0, width)], preferred_element_type=jnp.float32)
        for r in range(1, OCC):
            total += jnp.dot(part(r), amp[pl.ds(r * width, width)], preferred_element_type=jnp.float32)
        for i in range(own):
            outgoing[k, i, rows] = total[:, i * VBLK : (i + 1) * VBLK].astype(jnp.bfloat16)

    depth = b_ref.shape[1]
    half = depth // 32 * 16
    back = {}
    for k in far_first:
        for c, rows in enumerate((pl.ds(0, half), pl.ds(half, depth - half))):
            density(k, rows)
            back[k, c] = remote(
                outgoing.at[k, :, rows], out_ref.at[z, :, rows], r_send.at[k, c], r_recv.at[k, c], aux=zs[k]
            )
            back[k, c].start()
    density(0, pl.ds(0, depth))
    store = pltpu.make_async_copy(outgoing.at[0], out_ref.at[z], store_sem)
    store.start()

    for copy in back.values():
        copy.wait_recv()

    for piece in pieces:
        near[piece].wait_send()
        cross[piece].wait_send()
        onward[piece].wait_send()
        if piece[0]:
            z_copies[piece].wait_send()
    for copy in back.values():
        copy.wait_send()
    store.wait()


def shards(n, b_factors, tile_mask, batch_list, occ_energy, vir_energy):
    own, depth, columns = b_factors.shape
    width = own * VBLK
    dma = pltpu.SemaphoreType.DMA
    chunk = (own, depth, VBLK)
    chunk_bytes = own * depth * VBLK * 2
    pair_bytes = OCC * width * width * 4
    need = (OCC + 2) * n * chunk_bytes + 4 * pair_bytes + 2 * n * chunk_bytes
    hbm = pl.BlockSpec(memory_space=pltpu.HBM)
    slots = pl.pallas_call(
        functools.partial(kernel, n),
        out_shape=jax.ShapeDtypeStruct((n,) + chunk, jnp.bfloat16),
        in_specs=[hbm] * 5,
        out_specs=hbm,
        scratch_shapes=[
            pltpu.SMEM(tile_mask.shape, jnp.int32),
            pltpu.SMEM(batch_list.shape, jnp.int32),
            pltpu.SMEM(occ_energy.shape, jnp.float32),
            pltpu.VMEM((1, VBLK), jnp.float32),
            pltpu.VMEM((OCC, n) + chunk, jnp.bfloat16),
            pltpu.VMEM((width, OCC * width), jnp.float32),
            pltpu.VMEM((OCC * width, width), jnp.float32),
            pltpu.VMEM((OCC * width, width), jnp.float32),
            pltpu.VMEM((OCC * width, width), jnp.bfloat16),
            pltpu.VMEM((n,) + chunk, jnp.bfloat16),
            dma,
            dma((4,)),
            dma((n, own)),
            dma((n, own)),
            dma((3, n, own)),
            dma((3, n, own)),
            dma((n, 2)),
            dma((n, 2)),
            dma,
        ],
        compiler_params=pltpu.CompilerParams(
            collective_id=0, has_side_effects=True, vmem_limit_bytes=58000 << 10
        ),
    )(b_factors, tile_mask, batch_list, occ_energy, vir_energy[None, :])
    return jnp.concatenate([slots[k].astype(jnp.float32) for k in range(n)], axis=2)


def solution(mesh):
    in_specs = (P(("grp", "occ"), "aux", None), P("grp", None), P("grp"), P(), P("aux"))
    out_specs = P(("grp", "occ"), "aux", None)
    return jax.shard_map(
        functools.partial(shards, mesh.shape["aux"]), mesh=mesh, in_specs=in_specs, out_specs=out_specs, check_vma=False
    )
```
